128 devices in a mesh: context: 2 (over core), experts: 64 (over x, z, y).
Axes of the slice: x: 4, y: 4, z: 4, core: 2. Of those that a mesh axis runs over, the one named last changes fastest.
Arguments:
- inputs: bfloat16 [64, 2, 2, 112, 768], P('experts', 'context'), may hold values from -6 to 6
- counts: int32 [64, 2, 2], P('experts', 'context'), may hold values from 85 to 112, as said below
- routes: int32 [64, 2, 2, 112, 2], P('experts', 'context'), may hold values from 0 to 63, all different within a row; in each aligned block of 224 rows (0 to 223, 224 to 447, ..., all dimensions but the last counted through in order) at most 8 rows name the same one
- cotangent: bfloat16 [64, 2, 2, 112, 768], P('experts', 'context'), may hold values from -6 to 6
- gain1: bfloat16 [768], P(('context', 'experts')), may hold values from 0.5 to 1.5
- bias1: bfloat16 [768], P(('context', 'experts')), may hold values from -0.59765625 to 0.59765625
- project1: bfloat16 [768, 2304], P(('context', 'experts')), may hold values from -0.21875 to 0.21875
- output1: bfloat16 [768, 768], P(('context', 'experts')), may hold values from -2 to 2
- offset1: bfloat16 [768], P(('context', 'experts')), may hold values from -0.59765625 to 0.59765625
- gain2: bfloat16 [768], P(('context', 'experts')), may hold values from 0.5 to 1.5
- bias2: bfloat16 [768], P(('context', 'experts')), may hold values from -0.59765625 to 0.59765625
- expand: bfloat16 [768, 3072], P(('context', 'experts')), may hold values from -0.21875 to 0.21875
- expand_bias: bfloat16 [3072], P(('context', 'experts')), may hold values from -0.59765625 to 0.59765625
- shrink: bfloat16 [3072, 768], P(('context', 'experts')), may hold values from -0.15625 to 0.15625
- shrink_bias: bfloat16 [768], P(('context', 'experts')), may hold values from -0.59765625 to 0.59765625
- gain3: bfloat16 [768], P(('context', 'experts')), may hold values from 0.5 to 1.5
- bias3: bfloat16 [768], P(('context', 'experts')), may hold values from -0.59765625 to 0.59765625
- project2: bfloat16 [768, 2304], P(('context', 'experts')), may hold values from -0.21875 to 0.21875
- output2: bfloat16 [768, 768], P(('context', 'experts')), may hold values from -2 to 2
- offset2: bfloat16 [768], P(('context', 'experts')), may hold values from -2.390625 to 2.390625
- gain4: bfloat16 [768], P(('context', 'experts')), may hold values from 0.5 to 1.5
- bias4: bfloat16 [768], P(('context', 'experts')), may hold values from -0.59765625 to 0.59765625
- router: bfloat16 [768, 64], P(('context', 'experts')), may hold values from -0.15625 to 0.15625
- hidden_weight: bfloat16 [64, 768, 3072], P('experts', None, 'context'), may hold values from -0.21875 to 0.21875
- hidden_bias: bfloat16 [64, 3072], P('experts', 'context'), may hold values from -0.59765625 to 0.59765625
- return_weight: bfloat16 [64, 3072, 768], P('experts', 'context'), may hold values from -0.15625 to 0.15625
- return_bias: bfloat16 [64, 768], P('experts'), may hold values from -0.59765625 to 0.59765625
Outputs:
- outputs: bfloat16 [64, 2, 2, 112, 768], P('experts', 'context')
- inputs_grad: float32 [64, 2, 2, 112, 768], P('experts', 'context')
- gain1_grad: float32 [768], P(('context', 'experts'))
- bias1_grad: float32 [768], P(('context', 'experts'))
- project1_grad: float32 [768, 2304], P(('context', 'experts'))
- output1_grad: float32 [768, 768], P(('context', 'experts'))
- offset1_grad: float32 [768], P(('context', 'experts'))
- gain2_grad: float32 [768], P(('context', 'experts'))
- bias2_grad: float32 [768], P(('context', 'experts'))
- expand_grad: float32 [768, 3072], P(('context', 'experts'))
- expand_bias_grad: float32 [3072], P(('context', 'experts'))
- shrink_grad: float32 [3072, 768], P(('context', 'experts'))
- shrink_bias_grad: float32 [768], P(('context', 'experts'))
- gain3_grad: float32 [768], P(('context', 'experts'))
- bias3_grad: float32 [768], P(('context', 'experts'))
- project2_grad: float32 [768, 2304], P(('context', 'experts'))
- output2_grad: float32 [768, 768], P(('context', 'experts'))
- offset2_grad: float32 [768], P(('context', 'experts'))
- gain4_grad: float32 [768], P(('context', 'experts'))
- bias4_grad: float32 [768], P(('context', 'experts'))
- router_grad: float32 [768, 64], P(('context', 'experts'))
- hidden_weight_grad: float32 [64, 768, 3072], P('experts', None, 'context')
- hidden_bias_grad: float32 [64, 3072], P('experts', 'context')
- return_weight_grad: float32 [64, 3072, 768], P('experts', 'context')
- return_bias_grad: float32 [64, 768], P('experts')
The draws below stay inside these ranges and needn't reach their ends.
Inputs may be any that keep to these rules, and one draw needn't show every extreme that they name: counts[g, 0, j] + counts[g, 1, j] = 197; some image has the most on side 0 and some on side 1. `routes`: A row names two different experts; among the rows of one device no expert is named more than 8 times, and some device names one expert exactly 8 times.
All inputs are finite; a program needn't handle non-finite values.
Results may differ from the reference program's by a relative error of at most 0.03.
Values may be sent and summed in bfloat16 or wider, within the bound.
No kernel may reach another device: no remote copies, remote signals or barrier semaphores. Data moves between devices by JAX's collectives and lax.ppermute only.
A program may use at most 192 MiB of HBM per device.

```python
import math
import jax
import jax.numpy as jnp
import numpy as np
from jax import lax

D = 768
HEAD = 64
FF = 3072
SEQ = 197
SLOT = 112
IMG_DEV = 2
GROUPS = 64
SIDES = 2
EXPERTS = 64
CAP = 8


def draw_counts(key, part):
    key = jax.random.fold_in(key, 7)
    first, second = jax.random.split(key)
    total = GROUPS * IMG_DEV
    share = jax.random.randint(first, (total,), SEQ - SLOT, SLOT + 1, dtype=jnp.int32)
    order = jax.random.permutation(second, total)
    share = share.at[order[0]].set(SLOT).at[order[1]].set(SEQ - SLOT)
    share = share.reshape(GROUPS, IMG_DEV)
    return jnp.stack([share, SEQ - share], axis=1)


def shard_levels(stream_key, shape, shards, low, largest):
    factor_of = 1.0
    for dim, shards_of in shards:
        draws = jax.random.uniform(jax.random.fold_in(jax.random.fold_in(stream_key, 6), dim), (shards_of,), jnp.float32, low / len(shards), largest / len(shards))
        factor_of = factor_of * jnp.repeat(jnp.exp(draws), shape[dim] // shards_of).reshape((-1,) + (1,) * (len(shape) - 1 - dim))
    return factor_of


def shared_out(stream_key, own, number, rows, count, top, most, slope):
    order = jax.random.permutation(stream_key, count)
    heavy_load, ordinary = portions_of(count, rows * top, most, slope, True), portions_of(count, rows * top, most, slope, False)
    places = jnp.arange(count)

    def named(lengths, offset_by):
        used = int((lengths > 0).sum())
        fixed = max(1, used // 4)
        passed = fixed + (places - fixed + offset_by * (used - fixed)) % max(1, count - fixed)
        return jnp.zeros((count,), jnp.int32).at[order[jnp.where(places < fixed, places, passed)]].set(jnp.asarray(lengths, jnp.int32))

    lengths = jnp.where(number % 4 == 0, named(heavy_load, number // 4), named(ordinary, number - number // 4 - 1))
    mixed = jax.random.permutation(jax.random.fold_in(own, 3), count)
    source_of, sink = mixed[0:count // 2 * 2:2], mixed[1:count // 2 * 2:2]
    room = jnp.minimum(lengths[source_of] - 1, most - lengths[sink]) // 2
    room = jnp.where((source_of == order[0]) | (sink == order[0]) | (lengths[sink] == 0), 0, jnp.maximum(room, 0))
    passed = jax.random.randint(jax.random.fold_in(own, 4), (count // 2,), 0, 1 << 20) % (room + 1)
    lengths = lengths.at[source_of].add(-passed).at[sink].add(passed)
    items = jnp.searchsorted(jnp.cumsum(lengths), jnp.arange(rows * top), side="right").astype(jnp.int32)
    grid = items.reshape(top, rows).T
    grid = grid[jax.random.permutation(jax.random.fold_in(own, 1), rows)]
    offset_by = jax.random.randint(jax.random.fold_in(own, 2), (rows, 1), 0, top)
    return jnp.take_along_axis(grid, (jnp.arange(top)[None, :] + offset_by) % top, axis=1)


def portions_of(count, total, bound, lean, full):
    portions = [(1 << 20) // math.isqrt(standing ** lean) + 1 for standing in range(1, count + 1)]
    largest = bound if full else min(bound, max(-(-total // count), total * portions[0] // sum(portions)))
    least = 1 if total - largest >= count - 1 else 0
    holding, surplus = [largest] + [least] * (count - 1), total - largest - least * (count - 1)
    while surplus > 0:
        candidates = [i for i in range(1, count) if holding[i] < largest] or [i for i in range(1, count) if holding[i] < bound]
        whole, left = sum([portions[i] for i in candidates]), surplus
        for i in candidates:
            extra = min(bound - holding[i], max(1, left * portions[i] // whole), surplus)
            holding[i] = holding[i] + extra
            surplus = surplus - extra
    return np.array(holding)


def bell_draw(stream_key, extent, scale, most, cuts=(), held_as=jnp.bfloat16):
    values = scale * jax.random.normal(stream_key, extent, jnp.float32)
    if cuts:
        values = values * shard_levels(stream_key, extent, cuts, -0.22, 0.18)
    return jnp.clip(values, -most, most).astype(held_as)


def setup_inputs(seed: int = 0) -> dict:
    splits = jax.random.split(jax.random.key(seed), 28)
    inputs = bell_draw(splits[0], (GROUPS, SIDES, IMG_DEV, SLOT, D), 1.0, 6.0, ((0, 64), (1, 2)))
    counts = draw_counts(jax.random.fold_in(splits[27], 71), 0)
    routes_keys = jax.random.split(jax.random.fold_in(splits[2], 1), GROUPS * SIDES * IMG_DEV * SLOT // (IMG_DEV * SLOT))
    routes_turns = jax.random.permutation(jax.random.fold_in(splits[2], 3), GROUPS * SIDES * IMG_DEV * SLOT // (IMG_DEV * SLOT))
    routes = jax.vmap(lambda own, number: shared_out(jax.random.fold_in(splits[2], 2), own, number, IMG_DEV * SLOT, EXPERTS, 2, CAP, 1))(routes_keys, routes_turns).reshape((GROUPS, SIDES, IMG_DEV, SLOT, 2))
    cotangent = bell_draw(splits[3], (GROUPS, SIDES, IMG_DEV, SLOT, D), 1.0, 6.0, ((0, 64), (1, 2)))
    gain1 = jnp.clip(1.0 + 0.1 * jax.random.normal(splits[4], (D,), jnp.float32), 0.5, 1.5).astype(jnp.bfloat16)
    bias1 = bell_draw(splits[5], (D,), 0.1, 0.59765625, ((0, 128),))
    project1 = bell_draw(splits[6], (D, 3 * D), D ** -0.5, 0.21875, ((0, 128),))
    output1 = bell_draw(splits[7], (D, D), (D // 96) ** -0.5, 2.0, ((0, 128),))
    offset1 = bell_draw(splits[8], (D,), 0.1, 0.59765625, ((0, 128),))
    gain2 = jnp.clip(1.0 + 0.1 * jax.random.normal(splits[9], (D,), jnp.float32), 0.5, 1.5).astype(jnp.bfloat16)
    bias2 = bell_draw(splits[10], (D,), 0.1, 0.59765625, ((0, 128),))
    expand = bell_draw(splits[11], (D, FF), D ** -0.5, 0.21875, ((0, 128),))
    expand_bias = bell_draw(splits[12], (FF,), 0.1, 0.59765625, ((0, 128),))
    shrink = bell_draw(splits[13], (FF, D), (FF // 2) ** -0.5, 0.15625, ((0, 128),))
    shrink_bias = bell_draw(splits[14], (D,), 0.1, 0.59765625, ((0, 128),))
    gain3 = jnp.clip(1.0 + 0.1 * jax.random.normal(splits[15], (D,), jnp.float32), 0.5, 1.5).astype(jnp.bfloat16)
    bias3 = bell_draw(splits[16], (D,), 0.1, 0.59765625, ((0, 128),))
    project2 = bell_draw(splits[17], (D, 3 * D), D ** -0.5, 0.21875, ((0, 128),))
    output2 = bell_draw(splits[18], (D, D), (D // 96) ** -0.5, 2.0, ((0, 128),))
    offset2 = bell_draw(splits[19], (D,), 0.4, 2.390625, ((0, 128),))
    gain4 = jnp.clip(1.0 + 0.1 * jax.random.normal(splits[20], (D,), jnp.float32), 0.5, 1.5).astype(jnp.bfloat16)
    bias4 = bell_draw(splits[21], (D,), 0.1, 0.59765625, ((0, 128),))
    router = bell_draw(splits[22], (D, EXPERTS), (2 * D) ** -0.5, 0.15625, ((0, 128),))
    hidden_weight = bell_draw(splits[23], (EXPERTS, D, FF), D ** -0.5, 0.21875, ((0, 64), (2, 2)))
    hidden_bias = bell_draw(splits[24], (EXPERTS, FF), 0.1, 0.59765625, ((0, 64), (1, 2)))
    return_weight = bell_draw(splits[25], (EXPERTS, FF, D), (FF // 2) ** -0.5, 0.15625, ((0, 64), (1, 2)))
    return_bias = bell_draw(splits[26], (EXPERTS, D), 0.1, 0.59765625, ((0, 64),))
    return {"inputs": inputs, "counts": counts, "routes": routes, "cotangent": cotangent, "gain1": gain1, "bias1": bias1, "project1": project1, "output1": output1, "offset1": offset1, "gain2": gain2, "bias2": bias2, "expand": expand, "expand_bias": expand_bias, "shrink": shrink, "shrink_bias": shrink_bias, "gain3": gain3, "bias3": bias3, "project2": project2, "output2": output2, "offset2": offset2, "gain4": gain4, "bias4": bias4, "router": router, "hidden_weight": hidden_weight, "hidden_bias": hidden_bias, "return_weight": return_weight, "return_bias": return_bias}


@jax.custom_vjp
def low(v):
    return lax.optimization_barrier(v.astype(jnp.bfloat16)).astype(jnp.float32)

@jax.custom_vjp
def low_back(v):
    return v

def low_keep(v):
    return (low(v), None)

def low_pass(kept, grad):
    return (grad,)

def back_keep(v):
    return (v, None)

def back_low(kept, grad):
    return (low(grad),)
low.defvjp(low_keep, low_pass)
low_back.defvjp(back_keep, back_low)
norm_eps = 1e-06
masked_score = -1000000000.0

def product(left, right):
    return jnp.dot(left, right, precision=lax.Precision.HIGHEST, preferred_element_type=jnp.float32)

def layer_norm(values, norm_gain, norm_bias):
    average = lax.optimization_barrier(jnp.mean(values, axis=-1, keepdims=True))
    centred = values - average
    variance = lax.optimization_barrier(jnp.mean(centred * centred, axis=-1, keepdims=True))
    return centred * lax.rsqrt(variance + norm_eps) * norm_gain + norm_bias

def attention(stream, key_valid, norm_gain, norm_bias, weight, out_weight, out_bias):
    images, length, width = stream.shape
    heads = width // HEAD
    normed = low(layer_norm(stream, norm_gain, norm_bias))
    mixed = low_back(low(product(normed, weight)))
    split = mixed.reshape(images, length, 3, heads, HEAD)
    query_heads = split[:, :, 0]
    key_heads = split[:, :, 1]
    value_heads = split[:, :, 2]
    scores = jnp.einsum('iqhc,ikhc->ihqk', query_heads, key_heads, precision=lax.Precision.HIGHEST) * HEAD ** (-0.5)
    scores = jnp.where(key_valid[:, None, None, :], scores, masked_score)
    scores = low_back(scores)
    weights = low(jax.nn.softmax(scores, axis=-1))
    attended = jnp.einsum('ihqk,ikhc->iqhc', weights, value_heads, precision=lax.Precision.HIGHEST)
    attended = low_back(low(attended.reshape(images, length, width)))
    return low_back(product(attended, out_weight) + out_bias)

def feed_forward(stream, norm_gain, norm_bias, expand, expand_bias, shrink, shrink_bias):
    normed = low(layer_norm(stream, norm_gain, norm_bias))
    before = low_back(product(normed, expand) + expand_bias)
    hidden = low(jax.nn.gelu(before, approximate=False))
    return low_back(product(hidden, shrink) + shrink_bias)

def lower_block(stream, key_valid, dense):
    stream = stream + attention(stream, key_valid, dense[0], dense[1], dense[2], dense[3], dense[4])
    stream = stream + feed_forward(stream, dense[5], dense[6], dense[7], dense[8], dense[9], dense[10])
    stream = stream + attention(stream, key_valid, dense[11], dense[12], dense[13], dense[14], dense[15])
    return (stream, low(layer_norm(stream, dense[16], dense[17])))

def expert_block(pieces):
    rows_in, weight_in, bias_in, weight_out, bias_out = pieces
    before = low_back(product(rows_in, weight_in) + bias_in)
    hidden = low(jax.nn.gelu(before, approximate=False))
    return low_back(low(product(hidden, weight_out) + bias_out))

def to_devices(values, groups, images, sides, slots, width):
    shaped = values.reshape(groups, images, sides, slots, width).transpose(0, 2, 1, 3, 4)
    return shaped.reshape(groups * sides, images * slots, width)

def forward(stream, dense, experts, key_valid, row_valid, routes):
    groups, sides, images, slots, width = stream.shape
    by_image = stream.transpose(0, 2, 1, 3, 4).reshape(groups, images, sides * slots, width)

    def one_group(pieces):
        return lower_block(pieces[0], pieces[1], dense)
    upper, normed = lax.map(jax.checkpoint(one_group), (by_image, key_valid))
    sources = groups * sides
    rows = images * slots
    upper = to_devices(upper, groups, images, sides, slots, width)
    normed = to_devices(normed, groups, images, sides, slots, width)
    router = dense[18]
    count_experts = router.shape[1]
    logits = low_back(jnp.einsum('srd,de->sre', normed, router, precision=lax.Precision.HIGHEST))
    chosen = routes.reshape(sources, rows, 2)
    hot = (chosen[:, :, :, None] == jnp.arange(count_experts, dtype=jnp.int32)).astype(jnp.float32)
    picked = lax.optimization_barrier(jnp.sum(hot * logits[:, :, None, :], axis=-1))
    gates = jax.nn.softmax(picked, axis=-1) * row_valid[:, :, None]
    pair_hot = (chosen.reshape(sources, 2 * rows, 1) == jnp.arange(count_experts, dtype=jnp.int32)).astype(jnp.int32)
    earlier = jnp.cumsum(pair_hot, axis=1) - pair_hot
    slot = lax.optimization_barrier(jnp.sum(earlier * pair_hot, axis=-1))
    position = chosen.reshape(sources, 2 * rows) * CAP + slot
    places = jnp.arange(count_experts * CAP, dtype=jnp.int32)
    dispatch = (places[None, :, None] == position[:, None, :]).astype(jnp.float32)
    row_dispatch = lax.optimization_barrier(jnp.sum(dispatch.reshape(sources, count_experts * CAP, rows, 2), axis=-1))
    sent = low_back(jnp.einsum('spr,srd->spd', row_dispatch, normed, precision=lax.Precision.HIGHEST))
    grouped = sent.reshape(sources, count_experts, CAP, width).transpose(1, 0, 2, 3)
    grouped = grouped.reshape(count_experts, sources * CAP, width)
    produced = lax.map(jax.checkpoint(expert_block), (grouped,) + experts)
    produced = produced.reshape(count_experts, sources, CAP, width).transpose(1, 0, 2, 3)
    produced = produced.reshape(sources, count_experts * CAP, width)
    pair_out = jnp.einsum('spq,spd->sqd', dispatch, produced, precision=lax.Precision.HIGHEST)
    pair_out = pair_out.reshape(sources, rows, 2, width)
    mixture = lax.optimization_barrier(jnp.sum(gates[:, :, :, None] * pair_out, axis=2))
    result = (upper + mixture) * row_valid[:, :, None]
    return result.reshape(groups, sides, images, slots, width)

def reference(inputs, counts, routes, cotangent, gain1, bias1, project1, output1, offset1, gain2, bias2, expand, expand_bias, shrink, shrink_bias, gain3, bias3, project2, output2, offset2, gain4, bias4, router, hidden_weight, hidden_bias, return_weight, return_bias):
    dense = tuple((item.astype(jnp.float32) for item in (gain1, bias1, project1, output1, offset1, gain2, bias2, expand, expand_bias, shrink, shrink_bias, gain3, bias3, project2, output2, offset2, gain4, bias4, router)))
    experts = tuple((item.astype(jnp.float32) for item in (hidden_weight, hidden_bias, return_weight, return_bias)))
    groups, sides, images, slots, width = inputs.shape
    slot_iota = jnp.arange(slots, dtype=jnp.int32)
    valid = slot_iota < counts[:, :, :, None]
    key_valid = valid.transpose(0, 2, 1, 3).reshape(groups, images, sides * slots)
    row_valid = valid.reshape(groups * sides, images * slots).astype(jnp.float32)

    def run(stream, weights, owned):
        return forward(stream, weights, owned, key_valid, row_valid, routes)
    outputs, pullback = jax.vjp(run, inputs.astype(jnp.float32), dense, experts)
    grad_inputs, grad_dense, grad_experts = pullback(cotangent.astype(jnp.float32))
    return (outputs.astype(jnp.bfloat16), grad_inputs, grad_dense[0], grad_dense[1], grad_dense[2], grad_dense[3], grad_dense[4], grad_dense[5], grad_dense[6], grad_dense[7], grad_dense[8], grad_dense[9], grad_dense[10], grad_dense[11], grad_dense[12], grad_dense[13], grad_dense[14], grad_dense[15], grad_dense[16], grad_dense[17], grad_dense[18], grad_experts[0], grad_experts[1], grad_experts[2], grad_experts[3])
```

```python
import jax
import jax.numpy as jnp
from jax import lax
from jax.sharding import PartitionSpec as P

HEAD = 64
SEQ = 197
NORM_EPS = 1e-06
MASKED = -1000000000.0
BF16 = jnp.bfloat16
F32 = jnp.float32
STRIDE = {"x": 16, "z": 4, "y": 1}


def matmul(left, right):
    return jnp.dot(left, right, preferred_element_type=F32)


def contract_rows(left, right):
    return lax.dot_general(left, right, (((0,), (0,)), ((), ())), preferred_element_type=F32)


def times_transpose(left, right):
    return lax.dot_general(left, right, (((1,), (1,)), ((), ())), preferred_element_type=F32)


def coordinate(axis):
    return (lax.axis_index("experts") // STRIDE[axis]) % 4


def shift(values, axis, step):
    stride = STRIDE[axis]
    pairs = []
    for index in range(64):
        at = (index // stride) % 4
        pairs.append((index, index + ((at + step) % 4 - at) * stride))
    return lax.ppermute(values, "experts", pairs)


def swap(values):
    return lax.ppermute(values, "context", [(0, 1), (1, 0)])


def gather_stage(block, axis, dim):
    me = coordinate(axis)
    shape = block.shape[:dim] + (4,) + block.shape[dim:]
    whole = jnp.zeros(shape, block.dtype)
    moved = [block] + [shift(block, axis, step) for step in (1, 2, 3)]
    for step, piece in enumerate(moved):
        whole = lax.dynamic_update_index_in_dim(whole, piece, (me + 4 - step) % 4, dim)
    return whole


def gather_small(block):
    rows = block.shape[0]
    me = coordinate("y")
    moved = jnp.concatenate([block] + [shift(block, "y", step) for step in (1, 2, 3)], axis=0)
    place = lax.broadcasted_iota(jnp.int32, (4 * rows, 4 * rows), 0)
    source = lax.broadcasted_iota(jnp.int32, (4 * rows, 4 * rows), 1)
    wanted = ((me + 4 - place // rows) % 4) * rows + place % rows
    return matmul((source == wanted).astype(BF16), moved).astype(BF16)


def join_sides(own, other, side):
    whole = jnp.zeros((2,) + own.shape, own.dtype)
    whole = lax.dynamic_update_index_in_dim(whole, own, side, 0)
    whole = lax.dynamic_update_index_in_dim(whole, other, 1 - side, 0)
    return whole.reshape((2 * own.shape[0],) + own.shape[1:])


def gather_rows(block, order):
    columns = block.shape[1]
    if order[0] == "y":
        block = gather_small(block)
        first = gather_stage(block, order[1], 0)
        half = gather_stage(first, order[2], 0 if order[2] == "x" else 1)
    else:
        half = gather_stage(gather_stage(gather_stage(block, "x", 0), "z", 1), "y", 2)
    return half.reshape(-1, columns)


def scatter_stage(blocks, axis, dim):
    me = coordinate(axis)
    total = lax.dynamic_index_in_dim(blocks, me, dim, keepdims=False).astype(F32)
    for step in (1, 2, 3):
        piece = lax.dynamic_index_in_dim(blocks, (me + step) % 4, dim, keepdims=False)
        total = total + shift(piece, axis, step).astype(F32)
    return total


def scatter_rows(own, other, order):
    half = (own + swap(other.astype(BF16)).astype(F32)).astype(BF16)
    columns = half.shape[1]
    rows = half.shape[0] // 64
    blocks = half.reshape(4, 4, 4, rows, columns)
    if order == "xzy":
        blocks = half.reshape(4, 16 * rows, columns)
        blocks = scatter_stage(blocks, "x", 0).astype(BF16)
        blocks = scatter_stage(blocks.reshape(4, 4 * rows, columns), "z", 0).astype(BF16)
        return scatter_stage(blocks.reshape(4, rows, columns), "y", 0)
    if order == "zxy":
        blocks = half.reshape(4, 4, 4 * rows, columns)
        blocks = scatter_stage(blocks, "z", 1).astype(BF16)
        blocks = scatter_stage(blocks, "x", 0).astype(BF16)
        return scatter_stage(blocks.reshape(4, rows, columns), "y", 0)
    blocks = half.reshape(4, 4, 4, rows, columns)
    blocks = scatter_stage(blocks, "y", 2).astype(BF16)
    blocks = scatter_stage(blocks, "z", 1).astype(BF16)
    return scatter_stage(blocks, "x", 0)


def by_side(left, side):
    half = left.shape[1] // 2
    own = lax.dynamic_slice_in_dim(left, side * half, half, 1)
    other = lax.dynamic_slice_in_dim(left, (1 - side) * half, half, 1)
    return own, other


def grad_job(pairs, side, order):
    owns, others = [], []
    for terms in pairs:
        own_sum, other_sum = None, None
        for left, right in terms:
            own, other = by_side(left, side)
            own, other = contract_rows(own, right), contract_rows(other, right)
            own_sum = own if own_sum is None else own_sum + own
            other_sum = other if other_sum is None else other_sum + other
        owns.append(own_sum)
        others.append(other_sum.astype(BF16))
    return scatter_rows(jnp.concatenate(owns, axis=1), jnp.concatenate(others, axis=1), order)


def column(values, at):
    rows = values.shape[0]
    ones = (lax.broadcasted_iota(jnp.int32, (rows, 128), 1) == at).astype(BF16)
    return (values.astype(BF16), ones)


def norm_forward(values, gain, bias):
    average = jnp.mean(values, axis=-1, keepdims=True)
    centred = values - average
    variance = jnp.mean(centred * centred, axis=-1, keepdims=True)
    scale = lax.rsqrt(variance + NORM_EPS)
    return (centred * scale * gain + bias).astype(BF16)


def norm_backward(values, upstream, gain):
    average = jnp.mean(values, axis=-1, keepdims=True)
    centred = values - average
    variance = jnp.mean(centred * centred, axis=-1, keepdims=True)
    scale = lax.rsqrt(variance + NORM_EPS)
    unit = centred * scale
    scaled = upstream * gain
    first = jnp.mean(scaled, axis=-1, keepdims=True)
    second = jnp.mean(scaled * unit, axis=-1, keepdims=True)
    return (scaled - first - unit * second) * scale, upstream * unit


def gelu_both(values):
    size = jnp.abs(values)
    bell = jnp.exp(-0.5 * values * values)
    t = 1.0 / (1.0 + (0.3275911 * 0.7071067811865476) * size)
    series = 1.061405429
    for term in (-1.453152027, 1.421413741, -0.284496736, 0.254829592):
        series = series * t + term
    tail = 0.5 * series * t * bell
    share = jnp.where(values >= 0, 1.0 - tail, tail)
    return values * share, share + values * bell * 0.3989422804014327


def score_block(query_heads, key_heads, key_valid):
    scores = jnp.einsum(
        "iqhc,ikhc->ihqk", query_heads, key_heads, preferred_element_type=F32
    ) * HEAD ** (-0.5)
    return jnp.where(key_valid[:, None, None, :], scores, MASKED)


def attend_forward(stream, key_valid, gain, bias, weight, out_weight, out_bias, images):
    rows, width = stream.shape
    slots, heads = rows // images, width // HEAD
    normed = norm_forward(stream, gain, bias)
    keyed = matmul(normed, weight[:, width:]).astype(BF16)
    other = swap(keyed)
    queries = matmul(normed, weight[:, :width]).astype(BF16)
    queries = queries.reshape(images, slots, heads, HEAD)
    paired = jnp.concatenate(
        [keyed.reshape(images, slots, 2, heads, HEAD), other.reshape(images, slots, 2, heads, HEAD)],
        axis=1,
    )
    scores = score_block(queries, paired[:, :, 0], key_valid)
    top = jnp.max(scores, axis=-1, keepdims=True)
    log_total = top + jnp.log(jnp.sum(jnp.exp(scores - top), axis=-1, keepdims=True))
    weights = jnp.exp(scores - log_total).astype(BF16)
    attended = jnp.einsum(
        "ihqk,ikhc->iqhc", weights, paired[:, :, 1], preferred_element_type=F32
    )
    attended = attended.astype(BF16).reshape(rows, width)
    branch = matmul(attended, out_weight) + out_bias
    return branch, (normed, queries, paired, log_total, attended)


def attend_backward(stream, grad, kept, key_valid, gain, weight, out_weight, images):
    normed, queries, paired, log_total, attended = kept
    rows, width = stream.shape
    slots, heads = rows // images, width // HEAD
    scale = HEAD ** (-0.5)
    low = grad.astype(BF16)
    grad_attended = (
        times_transpose(low, out_weight).astype(BF16).reshape(images, slots, heads, HEAD)
    )
    keys, values = paired[:, :, 0], paired[:, :, 1]
    probs = jnp.exp(score_block(queries, keys, key_valid) - log_total)
    weights = probs.astype(BF16)
    grad_values = jnp.einsum(
        "ihqk,iqhc->ikhc", weights, grad_attended, preferred_element_type=F32
    )
    grad_probs = jnp.einsum(
        "iqhc,ikhc->ihqk", grad_attended, values, preferred_element_type=F32
    )
    centre = jnp.sum(grad_probs * probs, axis=-1, keepdims=True)
    grad_scores = (probs * (grad_probs - centre)).astype(BF16)
    grad_queries = (
        jnp.einsum("ihqk,ikhc->iqhc", grad_scores, keys, preferred_element_type=F32) * scale
    )
    grad_keys = (
        jnp.einsum("ihqk,iqhc->ikhc", grad_scores, queries, preferred_element_type=F32) * scale
    )
    grad_pair = jnp.stack([grad_keys, grad_values], axis=2).reshape(images, 2, slots, 2 * width)
    arrived = swap(grad_pair[:, 1].astype(BF16)).astype(F32)
    summed = (grad_pair[:, 0] + arrived).reshape(rows, 2 * width)
    grad_mixed = jnp.concatenate([grad_queries.reshape(rows, width), summed], axis=-1).astype(BF16)
    grad_normed = times_transpose(grad_mixed, weight)
    grad_stream, unit_grad = norm_backward(stream, grad_normed, gain)
    job = [[(normed, grad_mixed)], [(attended, low)]]
    small = [low, unit_grad, grad_normed]
    return grad_stream, job, small


def on_device(
    inputs,
    counts,
    routes,
    cotangent,
    gain1,
    bias1,
    project1,
    output1,
    offset1,
    gain2,
    bias2,
    expand,
    expand_bias,
    shrink,
    shrink_bias,
    gain3,
    bias3,
    project2,
    output2,
    offset2,
    gain4,
    bias4,
    router,
    hidden_weight,
    hidden_bias,
    return_weight,
    return_bias,
):
    images, slots, width = inputs.shape[2:]
    rows = images * slots
    side = lax.axis_index("context")
    count_experts = router.shape[1]

    vectors = (gain1, bias1, offset1, gain2, bias2, shrink_bias, gain3, bias3, offset2, gain4, bias4)
    small = jnp.concatenate(
        [router]
        + [v[:, None] for v in vectors]
        + [jnp.zeros((6, 128 - count_experts - len(vectors)), BF16)],
        axis=1,
    )
    first = gather_rows(jnp.concatenate([project1, output1, small], axis=1), "yzx")
    second = gather_rows(expand, "yxz")
    third = gather_rows(
        jnp.concatenate([shrink, jnp.pad(expand_bias[:, None], ((0, 0), (0, 127)))], axis=1), "xzy"
    )
    fourth = gather_rows(jnp.concatenate([project2, output2], axis=1), "yzx")
    first_other = swap(first)
    mixer_one = join_sides(first[:, : 3 * width], first_other[:, : 3 * width], side)
    outer_one = join_sides(
        first[:, 3 * width : 4 * width], first_other[:, 3 * width : 4 * width], side
    )
    small_full = join_sides(first[:, 4 * width :], first_other[:, 4 * width :], side)
    expand_full = join_sides(second, swap(second), side)
    third_other = swap(third)
    shrink_full = join_sides(third[:, :width], third_other[:, :width], side)
    shift_full = join_sides(third[:, width:], third_other[:, width:], side)
    fourth_other = swap(fourth)
    mixer_two = join_sides(fourth[:, : 3 * width], fourth_other[:, : 3 * width], side)
    outer_two = join_sides(fourth[:, 3 * width :], fourth_other[:, 3 * width :], side)
    router_full = small_full[:, :count_experts]
    pick = (
        lax.broadcasted_iota(jnp.int32, (16, 128), 1)
        == lax.broadcasted_iota(jnp.int32, (16, 128), 0) + count_experts
    ).astype(BF16)
    lanes = times_transpose(pick, small_full)
    (
        gain_one,
        bias_one,
        offset_one,
        gain_two,
        bias_two,
        shrink_shift,
        gain_three,
        bias_three,
        offset_two,
        gain_four,
        bias_four,
    ) = [lanes[i : i + 1] for i in range(len(vectors))]
    first_lane = (lax.broadcasted_iota(jnp.int32, (8, 128), 1) == 0).astype(BF16)
    expand_shift = times_transpose(first_lane, shift_full)[:1]

    stream = inputs.reshape(rows, width).astype(F32)
    own_count = counts.reshape(images)
    both_counts = jnp.stack([own_count, SEQ - own_count], axis=1)
    slot_iota = jnp.arange(slots, dtype=jnp.int32)
    key_valid = (slot_iota[None, None, :] < both_counts[:, :, None]).reshape(images, 2 * slots)
    row_valid = (slot_iota[None, :] < own_count[:, None]).reshape(rows, 1)
    valid = row_valid.astype(F32)
    capacity = max(2, 2 * rows // count_experts + 1)
    places = count_experts * capacity
    chosen = routes.reshape(rows, 2)
    expert_iota = jnp.arange(count_experts, dtype=jnp.int32)
    hots = [chosen[:, k : k + 1] == expert_iota for k in range(2)]
    row_hot = (hots[0] | hots[1]).astype(BF16)
    earlier_rows = (
        lax.broadcasted_iota(jnp.int32, (rows, rows), 1)
        < lax.broadcasted_iota(jnp.int32, (rows, rows), 0)
    ).astype(BF16)
    earlier = matmul(earlier_rows, row_hot)
    place_iota = lax.broadcasted_iota(jnp.int32, (rows, places), 1)
    goes = []
    for k in range(2):
        slot = jnp.sum(jnp.where(hots[k], earlier, 0.0), axis=-1, keepdims=True).astype(jnp.int32)
        goes.append(place_iota == chosen[:, k : k + 1] * capacity + slot)
    dispatch = [g.astype(BF16) for g in goes]
    row_dispatch = (goes[0] | goes[1]).astype(BF16)

    branch, kept_one = attend_forward(
        stream, key_valid, gain_one, bias_one, mixer_one, outer_one, offset_one, images
    )
    after_one = stream + branch
    normed_two = norm_forward(after_one, gain_two, bias_two)
    hidden_two, slope_two = gelu_both(matmul(normed_two, expand_full) + expand_shift)
    hidden_two = hidden_two.astype(BF16)
    after_two = after_one + matmul(hidden_two, shrink_full) + shrink_shift
    branch, kept_three = attend_forward(
        after_two, key_valid, gain_three, bias_three, mixer_two, outer_two, offset_two, images
    )
    after_three = after_two + branch
    normed = norm_forward(after_three, gain_four, bias_four)
    logits = matmul(normed, router_full)
    picked = [
        jnp.sum(jnp.where(hots[k], logits, 0.0), axis=-1, keepdims=True) for k in range(2)
    ]
    top = jnp.maximum(picked[0], picked[1])
    powers = [jnp.exp(p - top) for p in picked]
    shares = [p / (powers[0] + powers[1]) for p in powers]
    gates = [s * valid for s in shares]

    low_four = jnp.where(row_valid, cotangent.reshape(rows, width), jnp.zeros((), BF16))
    grad_four = low_four.astype(F32)
    place_gate = jnp.sum(
        jnp.where(goes[0], gates[0], 0.0) + jnp.where(goes[1], gates[1], 0.0), axis=0
    )
    sent = contract_rows(row_dispatch, normed).astype(BF16)
    grad_sent = (contract_rows(row_dispatch, low_four) * place_gate[:, None]).astype(BF16)
    arrived = lax.all_to_all(
        jnp.concatenate([sent, grad_sent], axis=1).reshape(count_experts, capacity, 2 * width),
        "experts",
        split_axis=0,
        concat_axis=0,
        tiled=True,
    ).reshape(places, 2 * width)
    arrived = jnp.concatenate([arrived, swap(arrived)], axis=0)
    expert_rows, grad_rows = arrived[:, :width], arrived[:, width:]
    in_weight, out_weight = hidden_weight[0], return_weight[0]
    hidden, slope = gelu_both(matmul(expert_rows, in_weight) + hidden_bias[0].astype(F32))
    hidden = hidden.astype(BF16)
    grad_before = (slope * times_transpose(grad_rows, out_weight)).astype(BF16)
    result = jnp.concatenate(
        [matmul(hidden, out_weight), times_transpose(grad_before, in_weight)], axis=1
    )
    result = result[:places] + swap(result[places:].astype(BF16)).astype(F32)
    back = jnp.concatenate(
        [result[:, :width] + return_bias[0].astype(F32), result[:, width:]], axis=1
    ).astype(BF16)
    back = lax.all_to_all(
        back.reshape(count_experts, capacity, 2 * width),
        "experts",
        split_axis=0,
        concat_axis=0,
        tiled=True,
    ).reshape(places, 2 * width)
    grad_return_bias = jnp.sum(grad_rows.astype(F32), axis=0)
    grad_return = contract_rows(hidden, grad_rows)
    grad_hidden_bias = jnp.sum(grad_before.astype(F32), axis=0)
    grad_hidden_weight = contract_rows(expert_rows, grad_before)
    pair_out = [matmul(dispatch[k], back[:, :width]) for k in range(2)]
    mixture = gates[0] * pair_out[0] + gates[1] * pair_out[1]
    outputs = ((after_three + mixture) * valid).astype(BF16).reshape(inputs.shape)

    grad_gates = [jnp.sum(grad_four * pair_out[k], axis=-1, keepdims=True) for k in range(2)]
    centre = shares[0] * grad_gates[0] + shares[1] * grad_gates[1]
    grad_picked = [valid * shares[k] * (grad_gates[k] - centre) for k in range(2)]
    grad_logits = (
        jnp.where(hots[0], grad_picked[0], 0.0) + jnp.where(hots[1], grad_picked[1], 0.0)
    ).astype(BF16)
    grad_normed = times_transpose(grad_logits, router_full) + matmul(
        row_dispatch, back[:, width:]
    )
    grad_flat, unit_four = norm_backward(after_three, grad_normed, gain_four)
    grad_three = grad_four + grad_flat
    wide_logits = jnp.pad(grad_logits, ((0, 0), (0, 128 - count_experts)))

    grad_part, job_a, small_a = attend_backward(
        after_two, grad_three, kept_three, key_valid, gain_three, mixer_two, outer_two, images
    )
    extra = [unit_four, grad_normed] + small_a
    job_a.append(
        [(normed, wide_logits)] + [column(v, count_experts + i) for i, v in enumerate(extra)]
    )
    sum_a = grad_job(job_a, side, "xzy")
    grad_two = grad_three + grad_part

    low_two = grad_two.astype(BF16)
    grad_before_two = (slope_two * times_transpose(low_two, shrink_full)).astype(BF16)
    sum_b = grad_job([[(hidden_two, low_two)], [column(grad_before_two, 0)]], side, "yzx")
    grad_normed_two = times_transpose(grad_before_two, expand_full)
    grad_part, unit_two = norm_backward(after_one, grad_normed_two, gain_two)
    sum_c = grad_job(
        [
            [(normed_two, grad_before_two)],
            [column(v, i) for i, v in enumerate([low_two, unit_two, grad_normed_two])],
        ],
        side,
        "zxy",
    )
    grad_one = grad_two + grad_part

    grad_part, job_d, small_d = attend_backward(
        stream, grad_one, kept_one, key_valid, gain_one, mixer_one, outer_one, images
    )
    job_d.append([column(v, i) for i, v in enumerate(small_d)])
    sum_d = grad_job(job_d, side, "xzy")
    grad_inputs = (grad_one + grad_part).reshape(inputs.shape)

    wide = 4 * width
    return (
        outputs,
        grad_inputs,
        sum_d[:, wide + 1],
        sum_d[:, wide + 2],
        sum_d[:, : 3 * width],
        sum_d[:, 3 * width : wide],
        sum_d[:, wide],
        sum_c[:, wide + 1],
        sum_c[:, wide + 2],
        sum_c[:, :wide],
        sum_b[:, width],
        sum_b[:, :width],
        sum_c[:, wide],
        sum_a[:, wide + 67],
        sum_a[:, wide + 68],
        sum_a[:, : 3 * width],
        sum_a[:, 3 * width : wide],
        sum_a[:, wide + 66],
        sum_a[:, wide + 64],
        sum_a[:, wide + 65],
        sum_a[:, wide : wide + 64],
        grad_hidden_weight[None],
        grad_hidden_bias[None],
        grad_return[None],
        grad_return_bias[None],
    )


def solution(mesh):
    vector = P(("context", "experts"))
    matrix = P(("context", "experts"), None)
    token = P("experts", "context", None, None, None)
    expert = (
        P("experts", None, "context"),
        P("experts", "context"),
        P("experts", "context", None),
        P("experts", None),
    )
    dense = (
        (vector, vector, matrix, matrix, vector)
        + (vector, vector, matrix, vector, matrix, vector)
        + (vector, vector, matrix, matrix, vector)
        + (vector, vector, matrix)
    )
    return jax.shard_map(
        on_device,
        mesh=mesh,
        in_specs=(token, P("experts", "context", None), token, token) + dense + expert,
        out_specs=(token, token) + dense + expert,
        check_vma=False,
    )
```

```python
import jax
import jax.numpy as jnp
from jax import lax
from jax.experimental import pallas as pl
from jax.experimental.pallas import tpu as pltpu
from jax.sharding import Mesh
from jax.sharding import PartitionSpec as P

HEAD = 64
SEQ = 197
NORM_EPS = 1e-06
MASKED = -1000000000.0
BF16 = jnp.bfloat16
F32 = jnp.float32


def matmul(left, right):
    return jnp.dot(left, right, preferred_element_type=F32)


def contract_rows(left, right):
    return lax.dot_general(left, right, (((0,), (0,)), ((), ())), preferred_element_type=F32)


def times_transpose(left, right):
    return lax.dot_general(left, right, (((1,), (1,)), ((), ())), preferred_element_type=F32)


def coordinate(axis):
    return lax.axis_index(axis)


def shift(values, axis, step):
    return lax.ppermute(values, axis, [(i, (i + step) % 4) for i in range(4)])


def swap(values):
    return lax.ppermute(values, "context", [(0, 1), (1, 0)])


def gather_stage(block, axis, dim):
    me = coordinate(axis)
    shape = block.shape[:dim] + (4,) + block.shape[dim:]
    whole = jnp.zeros(shape, block.dtype)
    moved = [block] + [shift(block, axis, step) for step in (1, 2, 3)]
    for step, piece in enumerate(moved):
        whole = lax.dynamic_update_index_in_dim(whole, piece, (me + 4 - step) % 4, dim)
    return whole


def gather_small(block):
    rows = block.shape[0]
    me = coordinate("y")
    moved = jnp.concatenate([block] + [shift(block, "y", step) for step in (1, 2, 3)], axis=0)
    place = lax.broadcasted_iota(jnp.int32, (4 * rows, 4 * rows), 0)
    source = lax.broadcasted_iota(jnp.int32, (4 * rows, 4 * rows), 1)
    wanted = ((me + 4 - place // rows) % 4) * rows + place % rows
    return matmul((source == wanted).astype(BF16), moved).astype(BF16)


def join_sides(own, other, side):
    whole = jnp.zeros((2,) + own.shape, own.dtype)
    whole = lax.dynamic_update_index_in_dim(whole, own, side, 0)
    whole = lax.dynamic_update_index_in_dim(whole, other, 1 - side, 0)
    return whole.reshape((2 * own.shape[0],) + own.shape[1:])


def gather_rest(block, order):
    first = gather_stage(block, order[0], 0)
    half = gather_stage(first, order[1], 0 if order[1] == "x" else 1)
    return half.reshape(-1, block.shape[1])


def exchange(values, axis, second):
    pairs = []
    for core in range(2):
        for at in range(4):
            to = at ^ 1 if (core == 0) != second else 3 - at
            pairs.append((4 * core + at, 4 * core + to))
    return lax.ppermute(values, ("context", axis), pairs)


def partners(axis):
    me = lax.axis_index(axis)
    near, far = jnp.bitwise_xor(me, 1), 3 - me
    core = lax.axis_index("context")
    return me, jnp.where(core == 0, near, far), jnp.where(core == 0, far, near)


def scatter_first(blocks, axis, dim):
    me, first, second = partners(axis)
    take = lambda at: lax.dynamic_index_in_dim(blocks, at, dim, keepdims=False)
    arrived = exchange(jnp.stack([take(first), take(jnp.bitwise_xor(me, 2))]), axis, False)
    own = take(me).astype(F32) + arrived[0].astype(F32)
    other = take(second).astype(F32) + arrived[1].astype(F32)
    return jnp.stack([own.astype(BF16), other.astype(BF16)])


def scatter_second(pair, axis):
    return pair[0].astype(F32) + exchange(pair[1], axis, True).astype(F32)


def own_half(values, side):
    half = values.shape[1] // 2
    return lax.dynamic_slice_in_dim(values, side * half, half, 1)


def both_rows(own, other):
    return jnp.concatenate([own, other], axis=0)


class Job:
    def __init__(self, parts, order):
        self.now = jnp.concatenate([p.astype(BF16) for p in parts], axis=1)
        self.order, self.stage = order, 0
        self.rows = self.now.shape[0] // 64

    def step(self):
        order, rows, columns = self.order, self.rows, self.now.shape[-1]
        axis = order[self.stage // 2]
        if self.stage % 2 == 0:
            left = [a for a in "xzy" if a not in order[: self.stage // 2]]
            dim = left.index(axis)
            shape = (4,) * dim + (4, 4 ** (len(left) - dim - 1) * rows, columns)
            self.now = scatter_first(self.now.reshape(shape), axis, dim)
        else:
            now = scatter_second(self.now, axis)
            self.now = (now if self.stage == 5 else now.astype(BF16)).reshape(-1, columns)
        self.stage += 1
        return self


def tie_jobs(value, *jobs):
    out = lax.optimization_barrier((value,) + tuple(job.now for job in jobs))
    for job, now in zip(jobs, out[1:]):
        job.now = now
    return out[0]


def row_sums(values, side):
    rows = values[0].shape[0]
    shape = (len(values) * rows, 128)
    ones = (
        lax.broadcasted_iota(jnp.int32, shape, 1)
        == lax.broadcasted_iota(jnp.int32, shape, 0) // rows
    ).astype(BF16)
    sums = contract_rows(jnp.concatenate([v.astype(BF16) for v in values], axis=0), ones)
    half = sums.shape[0] // 2
    own = lax.dynamic_slice_in_dim(sums, side * half, half, 0)
    other = lax.dynamic_slice_in_dim(sums, (1 - side) * half, half, 0)
    return own + swap(other.astype(BF16)).astype(F32)


def norm_forward(values, gain, bias):
    average = jnp.mean(values, axis=-1, keepdims=True)
    centred = values - average
    variance = jnp.mean(centred * centred, axis=-1, keepdims=True)
    scale = lax.rsqrt(variance + NORM_EPS)
    return (centred * scale * gain + bias).astype(BF16)


def norm_backward(values, upstream, gain):
    average = jnp.mean(values, axis=-1, keepdims=True)
    centred = values - average
    variance = jnp.mean(centred * centred, axis=-1, keepdims=True)
    scale = lax.rsqrt(variance + NORM_EPS)
    unit = centred * scale
    scaled = upstream * gain
    first = jnp.mean(scaled, axis=-1, keepdims=True)
    second = jnp.mean(scaled * unit, axis=-1, keepdims=True)
    return (scaled - first - unit * second) * scale, upstream * unit


def gelu_both(values):
    size = jnp.abs(values)
    bell = jnp.exp(-0.5 * values * values)
    t = 1.0 / (1.0 + (0.3275911 * 0.7071067811865476) * size)
    series = 1.061405429
    for term in (-1.453152027, 1.421413741, -0.284496736, 0.254829592):
        series = series * t + term
    tail = 0.5 * series * t * bell
    share = jnp.where(values >= 0, 1.0 - tail, tail)
    return values * share, share + values * bell * 0.3989422804014327


def head_pairs(values, lane_low):
    zero = jnp.zeros((), BF16)
    return jnp.concatenate([jnp.where(lane_low, values, zero), jnp.where(lane_low, zero, values)], axis=0)


def pair_probs(queries, keys, allowed):
    scores = jnp.where(allowed, times_transpose(queries, keys) * HEAD ** (-0.5), MASKED)
    powers = jnp.exp(scores - jnp.max(scores, axis=-1, keepdims=True))
    return powers / jnp.sum(powers, axis=-1, keepdims=True)


def key_mask(counts_ref, slots):
    image = pl.program_id(0)
    own = counts_ref[image]
    lane = lax.broadcasted_iota(jnp.int32, (2 * slots, 2 * slots), 1)
    return ((lane < slots) & (lane < own)) | ((lane >= slots) & (lane - slots < SEQ - own))


def attend_kernel(
    counts, q, kv, kv_other, weight, offset, stream, gain, bias, after, normed, attended
):
    slots, width = q.shape
    allowed = key_mask(counts, slots)
    lane_low = lax.broadcasted_iota(jnp.int32, (slots, 128), 1) < HEAD
    for at in range(0, width, 128):
        cut, value_cut = pl.ds(at, 128), pl.ds(width + at, 128)
        keys = jnp.concatenate([kv[:, cut], kv_other[:, cut]], axis=0)
        values = jnp.concatenate([kv[:, value_cut], kv_other[:, value_cut]], axis=0)
        probs = pair_probs(head_pairs(q[:, cut], lane_low), keys, allowed).astype(BF16)
        both = matmul(probs, values)
        attended[:, cut] = jnp.where(lane_low, both[:slots], both[slots:]).astype(BF16)
    total = stream[...] + matmul(attended[...], weight[...]) + offset[...]
    after[...] = total
    normed[...] = norm_forward(total, gain[...], bias[...])


def attend_back_kernel(counts, low, weight, q, kv, kv_other, grad_q, grad_own, grad_other):
    slots, width = q.shape
    allowed = key_mask(counts, slots)
    lane_low = lax.broadcasted_iota(jnp.int32, (slots, 128), 1) < HEAD
    scale = HEAD ** (-0.5)
    for at in range(0, width, 128):
        cut, value_cut = pl.ds(at, 128), pl.ds(width + at, 128)
        keys = jnp.concatenate([kv[:, cut], kv_other[:, cut]], axis=0)
        values = jnp.concatenate([kv[:, value_cut], kv_other[:, value_cut]], axis=0)
        queries = head_pairs(q[:, cut], lane_low)
        probs = pair_probs(queries, keys, allowed)
        grad_attended = head_pairs(
            times_transpose(low[...], weight[cut, :]).astype(BF16), lane_low
        )
        grad_values = contract_rows(probs.astype(BF16), grad_attended)
        grad_probs = times_transpose(grad_attended, values)
        centre = jnp.sum(grad_probs * probs, axis=-1, keepdims=True)
        grad_scores = (probs * (grad_probs - centre)).astype(BF16)
        both = matmul(grad_scores, keys)
        grad_q[:, cut] = (jnp.where(lane_low, both[:slots], both[slots:]) * scale).astype(BF16)
        grad_keys = contract_rows(grad_scores, queries) * scale
        grad_own[:, cut] = grad_keys[:slots]
        grad_own[:, value_cut] = grad_values[:slots]
        grad_other[:, cut] = grad_keys[slots:].astype(BF16)
        grad_other[:, value_cut] = grad_values[slots:].astype(BF16)


def row_block(slots, width):
    return pl.BlockSpec((slots, width), lambda i: (i, 0))


def whole_block(shape):
    return pl.BlockSpec(shape, lambda i: (0, 0))


PARAMS = pltpu.CompilerParams(vmem_limit_bytes=40 * 1024 * 1024)
COST = pl.CostEstimate(flops=1000000, bytes_accessed=100000, transcendentals=0)


def attend_forward(stream, normed, counts, wq, wkv, out_weight, out_bias, gain, bias):
    rows, width = stream.shape
    images = counts.shape[0]
    slots = rows // images
    keyed = matmul(normed, wkv).astype(BF16)
    other = swap(keyed)
    queries = matmul(normed, wq).astype(BF16)
    one, two = row_block(slots, width), row_block(slots, 2 * width)
    line = whole_block((1, width))
    after, next_normed, attended = pl.pallas_call(
        attend_kernel,
        grid=(images,),
        in_specs=[
            pl.BlockSpec(memory_space=pltpu.SMEM),
            one,
            two,
            two,
            whole_block((width, width)),
            line,
            one,
            line,
            line,
        ],
        out_specs=[one, one, one],
        out_shape=[
            jax.ShapeDtypeStruct((rows, width), F32),
            jax.ShapeDtypeStruct((rows, width), BF16),
            jax.ShapeDtypeStruct((rows, width), BF16),
        ],
        compiler_params=PARAMS,
        cost_estimate=COST,
        name="attend",
    )(counts, queries, keyed, other, out_weight, out_bias, stream, gain, bias)
    return after, next_normed, (queries, keyed, other, attended)


def attend_backward(stream, low, kept, counts, gain, wq, wkv, out_weight):
    queries, keyed, other, attended = kept
    rows, width = stream.shape
    images = counts.shape[0]
    slots = rows // images
    one, two = row_block(slots, width), row_block(slots, 2 * width)
    grad_q, grad_own, grad_other = pl.pallas_call(
        attend_back_kernel,
        grid=(images,),
        in_specs=[
            pl.BlockSpec(memory_space=pltpu.SMEM),
            one,
            whole_block((width, width)),
            one,
            two,
            two,
        ],
        out_specs=[one, two, two],
        out_shape=[
            jax.ShapeDtypeStruct((rows, width), BF16),
            jax.ShapeDtypeStruct((rows, 2 * width), F32),
            jax.ShapeDtypeStruct((rows, 2 * width), BF16),
        ],
        compiler_params=PARAMS,
        cost_estimate=COST,
        name="attend_back",
    )(counts, low, out_weight, queries, keyed, other)
    together = swap(jnp.concatenate([grad_q, grad_own.astype(BF16), grad_other], axis=1))
    partial = times_transpose(grad_q, wq)
    arrived = together[:, 3 * width :].astype(F32)
    grad_kv = (grad_own + arrived).astype(BF16)
    other_kv = (together[:, width : 3 * width].astype(F32) + grad_other.astype(F32)).astype(BF16)
    grad_normed = partial + times_transpose(grad_kv, wkv)
    grad_stream, unit_grad = norm_backward(stream, grad_normed, gain)
    both_q = both_rows(grad_q, together[:, :width])
    both_kv = both_rows(grad_kv, other_kv)
    return grad_stream, both_q, both_kv, unit_grad, grad_normed


def on_device(
    inputs,
    counts,
    routes,
    cotangent,
    gain1,
    bias1,
    project1,
    output1,
    offset1,
    gain2,
    bias2,
    expand,
    expand_bias,
    shrink,
    shrink_bias,
    gain3,
    bias3,
    project2,
    output2,
    offset2,
    gain4,
    bias4,
    router,
    hidden_weight,
    hidden_bias,
    return_weight,
    return_bias,
):
    images, slots, width = inputs.shape[2:]
    rows = images * slots
    side = lax.axis_index("context")
    count_experts = router.shape[1]

    vectors = (gain1, bias1, offset1, gain2, bias2, shrink_bias, gain3, bias3, offset2, gain4, bias4)
    count = len(vectors)
    small = jnp.concatenate(
        [
            router,
            jnp.concatenate(vectors).reshape(count, 6).T,
            jnp.zeros((6, 128 - count_experts - count), BF16),
        ],
        axis=1,
    )
    first_a = gather_small(project1)
    first_b = gather_small(jnp.concatenate([output1, small], axis=1))
    bulk = gather_small(jnp.concatenate([expand, project2, output2], axis=1))
    tall = gather_small(
        jnp.concatenate([shrink, jnp.pad(expand_bias[:, None], ((0, 0), (0, 127)))], axis=1)
    )
    tall_width = tall.shape[1]
    bulk = lax.all_gather(
        jnp.concatenate([bulk] + [tall[24 * q : 24 * q + 24] for q in range(4)], axis=1),
        ("context", "x", "z"),
        axis=0,
        tiled=True,
    )
    first_a = gather_rest(first_a, "zx")
    first_b = gather_rest(first_b, "xz")
    other_a, other_b = swap(first_a), swap(first_b)
    wq_one = join_sides(first_a[:, :width], other_a[:, :width], side)
    wkv_one = join_sides(first_a[:, width:], other_a[:, width:], side)
    outer_one = join_sides(first_b[:, :width], other_b[:, :width], side)
    small_full = join_sides(first_b[:, width:], other_b[:, width:], side)
    expand_full = bulk[:, : 4 * width]
    wq_two = bulk[:, 4 * width : 5 * width]
    wkv_two = bulk[:, 5 * width : 7 * width]
    outer_two = bulk[:, 7 * width : 8 * width]
    tall_cut = [
        bulk[:, 8 * width + q * tall_width : 8 * width + (q + 1) * tall_width].reshape(
            32, 24, tall_width
        )
        for q in range(4)
    ]
    shrink_full = jnp.stack([cut[:, :, :width] for cut in tall_cut], axis=1).reshape(-1, width)
    shift_full = jnp.stack([cut[:, :, width:] for cut in tall_cut], axis=1).reshape(-1, 128)
    router_full = small_full[:, :count_experts]
    pick = (
        lax.broadcasted_iota(jnp.int32, (16, 128), 1)
        == lax.broadcasted_iota(jnp.int32, (16, 128), 0) + count_experts
    ).astype(BF16)
    lanes = times_transpose(pick, small_full)
    (
        gain_one,
        bias_one,
        offset_one,
        gain_two,
        bias_two,
        shrink_shift,
        gain_three,
        bias_three,
        offset_two,
        gain_four,
        bias_four,
    ) = [lanes[i : i + 1] for i in range(count)]
    first_lane = (lax.broadcasted_iota(jnp.int32, (8, 128), 1) == 0).astype(BF16)
    expand_shift = times_transpose(first_lane, shift_full)[:1]

    stream = inputs.reshape(rows, width).astype(F32)
    own_count = counts.reshape(images)
    slot_iota = jnp.arange(slots, dtype=jnp.int32)
    row_valid = (slot_iota[None, :] < own_count[:, None]).reshape(rows, 1)
    valid = row_valid.astype(F32)
    capacity = max(2, 2 * rows // count_experts + 1)
    places = count_experts * capacity
    chosen = routes.reshape(rows, 2)
    expert_iota = jnp.arange(count_experts, dtype=jnp.int32)
    hots = [chosen[:, k : k + 1] == expert_iota for k in range(2)]
    row_hot = (hots[0] | hots[1]).astype(BF16)
    earlier_rows = (
        lax.broadcasted_iota(jnp.int32, (rows, rows), 1)
        < lax.broadcasted_iota(jnp.int32, (rows, rows), 0)
    ).astype(BF16)
    earlier = matmul(earlier_rows, row_hot)
    place_iota = lax.broadcasted_iota(jnp.int32, (rows, places), 1)
    goes = []
    for k in range(2):
        slot = jnp.sum(jnp.where(hots[k], earlier, 0.0), axis=-1, keepdims=True).astype(jnp.int32)
        goes.append(place_iota == chosen[:, k : k + 1] * capacity + slot)
    dispatch = [g.astype(BF16) for g in goes]
    row_dispatch = (goes[0] | goes[1]).astype(BF16)

    normed_one = norm_forward(stream, gain_one, bias_one)
    after_one, normed_two, kept_one = attend_forward(
        stream, normed_one, own_count, wq_one, wkv_one, outer_one, offset_one, gain_two, bias_two
    )
    hidden_two, slope_two = gelu_both(matmul(normed_two, expand_full) + expand_shift)
    hidden_two = hidden_two.astype(BF16)
    after_two = after_one + matmul(hidden_two, shrink_full) + shrink_shift
    normed_three = norm_forward(after_two, gain_three, bias_three)
    after_three, normed, kept_three = attend_forward(
        after_two,
        normed_three,
        own_count,
        wq_two,
        wkv_two,
        outer_two,
        offset_two,
        gain_four,
        bias_four,
    )
    halves = [normed_one, kept_one[3], normed_two, hidden_two, normed_three, kept_three[3], normed]
    arriving = swap(jnp.concatenate([own_half(v, 1 - side) for v in halves], axis=1))
    lefts, at = [], 0
    for v in halves:
        half = v.shape[1] // 2
        lefts.append(both_rows(own_half(v, side), arriving[:, at : at + half]))
        at += half
    left_one, left_out_one, left_two, left_hidden, left_three, left_out_three, left_four = lefts
    logits = matmul(normed, router_full)
    picked = [
        jnp.sum(jnp.where(hots[k], logits, 0.0), axis=-1, keepdims=True) for k in range(2)
    ]
    top = jnp.maximum(picked[0], picked[1])
    powers = [jnp.exp(p - top) for p in picked]
    shares = [p / (powers[0] + powers[1]) for p in powers]
    gates = [s * valid for s in shares]

    low_four = jnp.where(row_valid, cotangent.reshape(rows, width), jnp.zeros((), BF16))
    grad_four = low_four.astype(F32)
    place_gate = jnp.sum(
        jnp.where(goes[0], gates[0], 0.0) + jnp.where(goes[1], gates[1], 0.0), axis=0
    )
    sent = contract_rows(row_dispatch, normed).astype(BF16)
    grad_sent = (contract_rows(row_dispatch, low_four) * place_gate[:, None]).astype(BF16)
    arrived = lax.all_to_all(
        jnp.concatenate([sent, grad_sent], axis=1).reshape(count_experts, capacity, 2 * width),
        ("x", "z", "y"),
        split_axis=0,
        concat_axis=0,
        tiled=True,
    ).reshape(places, 2 * width)
    arrived = jnp.concatenate([arrived, swap(arrived)], axis=0)
    expert_rows, grad_rows = arrived[:, :width], arrived[:, width:]
    in_weight, out_weight = hidden_weight[0], return_weight[0]
    hidden, slope = gelu_both(matmul(expert_rows, in_weight) + hidden_bias[0].astype(F32))
    hidden = hidden.astype(BF16)
    grad_before = (slope * times_transpose(grad_rows, out_weight)).astype(BF16)
    result = jnp.concatenate(
        [matmul(hidden, out_weight), times_transpose(grad_before, in_weight)], axis=1
    )
    result = result[:places] + swap(result[places:].astype(BF16)).astype(F32)
    back = jnp.concatenate(
        [result[:, :width] + return_bias[0].astype(F32), result[:, width:]], axis=1
    ).astype(BF16)
    wide_back = lax.all_to_all(
        back.reshape(count_experts, capacity, 2 * width),
        ("x", "z", "y"),
        split_axis=0,
        concat_axis=0,
        tiled=True,
    ).reshape(places, 2 * width)
    grad_return_bias = jnp.sum(grad_rows.astype(F32), axis=0)
    grad_return = contract_rows(hidden, grad_rows)
    grad_hidden_bias = jnp.sum(grad_before.astype(F32), axis=0)
    grad_hidden_weight = contract_rows(expert_rows, grad_before)
    back, grad_return, grad_hidden_weight = lax.optimization_barrier(
        (wide_back, grad_return, grad_hidden_weight)
    )
    pair_out = [matmul(dispatch[k], back[:, :width]) for k in range(2)]
    mixture = gates[0] * pair_out[0] + gates[1] * pair_out[1]
    outputs = ((after_three + mixture) * valid).astype(BF16).reshape(inputs.shape)

    grad_gates = [jnp.sum(grad_four * pair_out[k], axis=-1, keepdims=True) for k in range(2)]
    centre = shares[0] * grad_gates[0] + shares[1] * grad_gates[1]
    grad_picked = [valid * shares[k] * (grad_gates[k] - centre) for k in range(2)]
    grad_logits = (
        jnp.where(hots[0], grad_picked[0], 0.0) + jnp.where(hots[1], grad_picked[1], 0.0)
    ).astype(BF16)
    grad_normed = times_transpose(grad_logits, router_full) + matmul(
        row_dispatch, back[:, width:]
    )
    grad_flat, unit_four = norm_backward(after_three, grad_normed, gain_four)
    grad_three = grad_four + grad_flat
    wide_logits = jnp.pad(grad_logits, ((0, 0), (0, 128 - count_experts)))

    low_three = grad_three.astype(BF16)
    low_logits = swap(jnp.concatenate([low_three, wide_logits], axis=1))
    grad_part, both_q, both_kv, unit_three, grad_normed_three = attend_backward(
        after_two, low_three, kept_three, own_count, gain_three, wq_two, wkv_two, outer_two
    )
    grad_two = grad_three + grad_part
    low_two = grad_two.astype(BF16)
    other_low_two = swap(low_two)
    sums_a = row_sums([unit_four, grad_normed, low_three, unit_three, grad_normed_three], side)
    job_a = Job(
        [
            contract_rows(left_three, both_q),
            contract_rows(left_three, both_kv),
            contract_rows(left_out_three, both_rows(low_three, low_logits[:, :width])),
            contract_rows(left_four, both_rows(wide_logits, low_logits[:, width:]))
            + jnp.roll(sums_a, count_experts, axis=1),
        ],
        "xzy",
    )
    low_two = tie_jobs(low_two, job_a)
    grad_before_two = (slope_two * times_transpose(low_two, shrink_full)).astype(BF16)
    other_before_two = swap(grad_before_two)
    sums_b = contract_rows(
        grad_before_two,
        (lax.broadcasted_iota(jnp.int32, (rows, 128), 1) == 0).astype(BF16),
    )
    half = sums_b.shape[0] // 2
    sums_b = lax.dynamic_slice_in_dim(sums_b, side * half, half, 0) + swap(
        lax.dynamic_slice_in_dim(sums_b, (1 - side) * half, half, 0).astype(BF16)
    ).astype(F32)
    job_b = Job([contract_rows(left_hidden, both_rows(low_two, other_low_two)), sums_b], "yzx")
    grad_before_two = tie_jobs(grad_before_two, job_b)
    grad_normed_two = times_transpose(grad_before_two, expand_full)
    grad_part, unit_two = norm_backward(after_one, grad_normed_two, gain_two)
    grad_one = grad_two + grad_part
    low_one = grad_one.astype(BF16)
    other_low_one = swap(low_one)
    job_c = Job(
        [
            contract_rows(left_two, both_rows(grad_before_two, other_before_two)),
            contract_rows(left_out_one, both_rows(low_one, other_low_one)),
            row_sums([low_two, unit_two, grad_normed_two, low_one], side),
        ],
        "zxy",
    )
    low_one = tie_jobs(low_one, job_c, job_a.step())
    grad_part, both_q, both_kv, unit_one, grad_normed_one = attend_backward(
        stream, low_one, kept_one, own_count, gain_one, wq_one, wkv_one, outer_one
    )
    both_q = tie_jobs(both_q, job_a.step(), job_b.step())
    job_e = Job([contract_rows(left_one, both_q), contract_rows(left_one, both_kv)], "xzy")
    job_f = Job([row_sums([unit_one, grad_normed_one], side)], "xzy")
    job_e.now = tie_jobs(job_e.now, job_a.step(), job_b.step(), job_c.step())
    tie_jobs(job_e.step().now, job_a.step(), job_b.step(), job_c.step(), job_f.step())
    tie_jobs(job_e.step().now, job_a.step(), job_b.step(), job_c.step(), job_f.step())
    job_e.now = jnp.concatenate([job_e.now, job_f.now], axis=1)
    tie_jobs(job_e.step().now, job_a.step(), job_b.step(), job_c.step())
    tie_jobs(job_e.step().now, job_b.step(), job_c.step())
    tie_jobs(job_e.step().now, job_c.step())
    job_e.step()
    sum_a, sum_b, sum_c, sum_e = job_a.now, job_b.now, job_c.now, job_e.now
    grad_inputs = (grad_one + grad_part).reshape(inputs.shape)

    wide = 4 * width
    return (
        outputs,
        grad_inputs,
        sum_e[:, 3 * width],
        sum_e[:, 3 * width + 1],
        sum_e[:, : 3 * width],
        sum_c[:, wide : wide + width],
        sum_c[:, wide + width + 3],
        sum_c[:, wide + width + 1],
        sum_c[:, wide + width + 2],
        sum_c[:, :wide],
        sum_b[:, width],
        sum_b[:, :width],
        sum_c[:, wide + width],
        sum_a[:, wide + 67],
        sum_a[:, wide + 68],
        sum_a[:, : 3 * width],
        sum_a[:, 3 * width : wide],
        sum_a[:, wide + 66],
        sum_a[:, wide + 64],
        sum_a[:, wide + 65],
        sum_a[:, wide : wide + 64],
        grad_hidden_weight[None],
        grad_hidden_bias[None],
        grad_return[None],
        grad_return_bias[None],
    )


def solution(mesh):
    chips = ("x", "z", "y")
    finer = Mesh(mesh.devices.reshape(2, 4, 4, 4), ("context",) + chips)
    vector = P(("context",) + chips)
    matrix = P(("context",) + chips, None)
    token = P(chips, "context", None, None, None)
    expert = (
        P(chips, None, "context"),
        P(chips, "context"),
        P(chips, "context", None),
        P(chips, None),
    )
    dense = (
        (vector, vector, matrix, matrix, vector)
        + (vector, vector, matrix, vector, matrix, vector)
        + (vector, vector, matrix, matrix, vector)
        + (vector, vector, matrix)
    )
    return jax.shard_map(
        on_device,
        mesh=finer,
        in_specs=(token, P(chips, "context", None), token, token) + dense + expert,
        out_specs=(token, token) + dense + expert,
        check_vma=False,
    )
```

```python
import jax
import jax.numpy as jnp
from jax import lax
from jax.experimental import pallas as pl
from jax.experimental.pallas import tpu as pltpu
from jax.sharding import Mesh
from jax.sharding import PartitionSpec as P

HEAD = 64
SEQ = 197
NORM_EPS = 1e-06
MASKED = -1000000000.0
BF16 = jnp.bfloat16
F32 = jnp.float32


def matmul(left, right):
    return jnp.dot(left, right, preferred_element_type=F32)


def contract_rows(left, right):
    return lax.dot_general(left, right, (((0,), (0,)), ((), ())), preferred_element_type=F32)


def times_transpose(left, right):
    return lax.dot_general(left, right, (((1,), (1,)), ((), ())), preferred_element_type=F32)


def coordinate(axis):
    return lax.axis_index(axis)


def shift(values, axis, step):
    return lax.ppermute(values, axis, [(i, (i + step) % 4) for i in range(4)])


def swap(values):
    return lax.ppermute(values, "context", [(0, 1), (1, 0)])


def exchange(values, axis, second):
    pairs = []
    for core in range(2):
        for at in range(4):
            to = at ^ 1 if (core == 0) != second else 3 - at
            pairs.append((4 * core + at, 4 * core + to))
    return lax.ppermute(values, ("context", axis), pairs)


def partners(axis):
    me = lax.axis_index(axis)
    near, far = jnp.bitwise_xor(me, 1), 3 - me
    core = lax.axis_index("context")
    return me, jnp.where(core == 0, near, far), jnp.where(core == 0, far, near)


def gather_stage(block, axis, dim):
    me = coordinate(axis)
    shape = block.shape[:dim] + (4,) + block.shape[dim:]
    whole = jnp.zeros(shape, block.dtype)
    moved = [block] + [shift(block, axis, step) for step in (1, 2, 3)]
    for step, piece in enumerate(moved):
        whole = lax.dynamic_update_index_in_dim(whole, piece, (me + 4 - step) % 4, dim)
    return whole


def gather_small(block):
    rows = block.shape[0]
    me = coordinate("y")
    moved = jnp.concatenate([block] + [shift(block, "y", step) for step in (1, 2, 3)], axis=0)
    place = lax.broadcasted_iota(jnp.int32, (4 * rows, 4 * rows), 0)
    source = lax.broadcasted_iota(jnp.int32, (4 * rows, 4 * rows), 1)
    wanted = ((me + 4 - place // rows) % 4) * rows + place % rows
    return matmul((source == wanted).astype(BF16), moved).astype(BF16)


def join_sides(own, other, side):
    whole = jnp.zeros((2,) + own.shape, own.dtype)
    whole = lax.dynamic_update_index_in_dim(whole, own, side, 0)
    whole = lax.dynamic_update_index_in_dim(whole, other, 1 - side, 0)
    return whole.reshape((2 * own.shape[0],) + own.shape[1:])


def gather_rest(block, order):
    first = gather_stage(block, order[0], 0)
    half = gather_stage(first, order[1], 0 if order[1] == "x" else 1)
    return half.reshape(-1, block.shape[1])


def scatter_first(blocks, axis, dim):
    me, first, second = partners(axis)
    take = lambda at: lax.dynamic_index_in_dim(blocks, at, dim, keepdims=False)
    arrived = exchange(jnp.stack([take(first), take(jnp.bitwise_xor(me, 2))]), axis, False)
    own = take(me).astype(F32) + arrived[0].astype(F32)
    other = take(second).astype(F32) + arrived[1].astype(F32)
    return jnp.stack([own.astype(BF16), other.astype(BF16)])


def scatter_second(pair, axis):
    return pair[0].astype(F32) + exchange(pair[1], axis, True).astype(F32)


def own_half(values, side):
    half = values.shape[1] // 2
    return lax.dynamic_slice_in_dim(values, side * half, half, 1)


def both_rows(own, other):
    return jnp.concatenate([own, other], axis=0)


class Job:
    def __init__(self, parts, order):
        self.now = jnp.concatenate([p.astype(BF16) for p in parts], axis=1)
        self.order, self.stage = order, 0
        self.rows = self.now.shape[0] // 64

    def step(self):
        order, rows, columns = self.order, self.rows, self.now.shape[-1]
        axis = order[self.stage // 2]
        if self.stage % 2 == 0:
            left = [a for a in "xzy" if a not in order[: self.stage // 2]]
            dim = left.index(axis)
            shape = (4,) * dim + (4, 4 ** (len(left) - dim - 1) * rows, columns)
            self.now = scatter_first(self.now.reshape(shape), axis, dim)
        else:
            now = scatter_second(self.now, axis)
            self.now = (now if self.stage == 5 else now.astype(BF16)).reshape(-1, columns)
        self.stage += 1
        return self


def tie_jobs(value, *jobs):
    out = lax.optimization_barrier((value,) + tuple(job.now for job in jobs))
    for job, now in zip(jobs, out[1:]):
        job.now = now
    return out[0]


def row_sums(values, side):
    rows = values[0].shape[0]
    shape = (len(values) * rows, 128)
    ones = (
        lax.broadcasted_iota(jnp.int32, shape, 1)
        == lax.broadcasted_iota(jnp.int32, shape, 0) // rows
    ).astype(BF16)
    sums = contract_rows(jnp.concatenate([v.astype(BF16) for v in values], axis=0), ones)
    half = sums.shape[0] // 2
    own = lax.dynamic_slice_in_dim(sums, side * half, half, 0)
    other = lax.dynamic_slice_in_dim(sums, (1 - side) * half, half, 0)
    return own + swap(other.astype(BF16)).astype(F32)


def norm_forward(values, gain, bias):
    average = jnp.mean(values, axis=-1, keepdims=True)
    centred = values - average
    variance = jnp.mean(centred * centred, axis=-1, keepdims=True)
    scale = lax.rsqrt(variance + NORM_EPS)
    return (centred * scale * gain + bias).astype(BF16)


def norm_backward(values, upstream, gain):
    average = jnp.mean(values, axis=-1, keepdims=True)
    centred = values - average
    variance = jnp.mean(centred * centred, axis=-1, keepdims=True)
    scale = lax.rsqrt(variance + NORM_EPS)
    unit = centred * scale
    scaled = upstream * gain
    first = jnp.mean(scaled, axis=-1, keepdims=True)
    second = jnp.mean(scaled * unit, axis=-1, keepdims=True)
    return (scaled - first - unit * second) * scale, upstream * unit


def gelu_both(values):
    size = jnp.abs(values)
    bell = jnp.exp(-0.5 * values * values)
    t = 1.0 / (1.0 + (0.3275911 * 0.7071067811865476) * size)
    series = 1.061405429
    for term in (-1.453152027, 1.421413741, -0.284496736, 0.254829592):
        series = series * t + term
    tail = 0.5 * series * t * bell
    share = jnp.where(values >= 0, 1.0 - tail, tail)
    return values * share, share + values * bell * 0.3989422804014327


def head_pairs(values, lane_low):
    zero = jnp.zeros((), BF16)
    return jnp.concatenate([jnp.where(lane_low, values, zero), jnp.where(lane_low, zero, values)], axis=0)


def pair_probs(queries, keys, allowed):
    scores = jnp.where(allowed, times_transpose(queries, keys) * HEAD ** (-0.5), MASKED)
    powers = jnp.exp(scores - jnp.max(scores, axis=-1, keepdims=True))
    return powers / jnp.sum(powers, axis=-1, keepdims=True)


def key_mask(counts_ref, slots):
    image = pl.program_id(0)
    own = counts_ref[image]
    lane = lax.broadcasted_iota(jnp.int32, (2 * slots, 2 * slots), 1)
    return ((lane < slots) & (lane < own)) | ((lane >= slots) & (lane - slots < SEQ - own))


def attend_kernel(
    counts, q, kv, kv_other, weight, offset, stream, gain, bias, after, normed, attended
):
    slots, width = q.shape
    allowed = key_mask(counts, slots)
    lane_low = lax.broadcasted_iota(jnp.int32, (slots, 128), 1) < HEAD
    for at in range(0, width, 128):
        cut, value_cut = pl.ds(at, 128), pl.ds(width + at, 128)
        keys = jnp.concatenate([kv[:, cut], kv_other[:, cut]], axis=0)
        values = jnp.concatenate([kv[:, value_cut], kv_other[:, value_cut]], axis=0)
        probs = pair_probs(head_pairs(q[:, cut], lane_low), keys, allowed).astype(BF16)
        both = matmul(probs, values)
        attended[:, cut] = jnp.where(lane_low, both[:slots], both[slots:]).astype(BF16)
    total = stream[...] + matmul(attended[...], weight[...]) + offset[...]
    after[...] = total
    normed[...] = norm_forward(total, gain[...], bias[...])


def attend_back_kernel(counts, low, weight, q, kv, kv_other, grad_q, grad_own, grad_other):
    slots, width = q.shape
    allowed = key_mask(counts, slots)
    lane_low = lax.broadcasted_iota(jnp.int32, (slots, 128), 1) < HEAD
    scale = HEAD ** (-0.5)
    for at in range(0, width, 128):
        cut, value_cut = pl.ds(at, 128), pl.ds(width + at, 128)
        keys = jnp.concatenate([kv[:, cut], kv_other[:, cut]], axis=0)
        values = jnp.concatenate([kv[:, value_cut], kv_other[:, value_cut]], axis=0)
        queries = head_pairs(q[:, cut], lane_low)
        probs = pair_probs(queries, keys, allowed)
        grad_attended = head_pairs(
            times_transpose(low[...], weight[cut, :]).astype(BF16), lane_low
        )
        grad_values = contract_rows(probs.astype(BF16), grad_attended)
        grad_probs = times_transpose(grad_attended, values)
        centre = jnp.sum(grad_probs * probs, axis=-1, keepdims=True)
        grad_scores = (probs * (grad_probs - centre)).astype(BF16)
        both = matmul(grad_scores, keys)
        grad_q[:, cut] = (jnp.where(lane_low, both[:slots], both[slots:]) * scale).astype(BF16)
        grad_keys = contract_rows(grad_scores, queries) * scale
        grad_own[:, cut] = grad_keys[:slots]
        grad_own[:, value_cut] = grad_values[:slots]
        grad_other[:, cut] = grad_keys[slots:].astype(BF16)
        grad_other[:, value_cut] = grad_values[slots:].astype(BF16)


def row_block(slots, width):
    return pl.BlockSpec((slots, width), lambda i: (i, 0))


def whole_block(shape):
    return pl.BlockSpec(shape, lambda i: (0, 0))


PARAMS = pltpu.CompilerParams(vmem_limit_bytes=40 * 1024 * 1024)
FORWARD_COST = pl.CostEstimate(flops=2000000000, bytes_accessed=8000000, transcendentals=0)
BACKWARD_COST = pl.CostEstimate(flops=9000000000, bytes_accessed=20000000, transcendentals=0)


def attend_forward(stream, normed, counts, wq, wkv, out_weight, out_bias, gain, bias):
    rows, width = stream.shape
    images = counts.shape[0]
    slots = rows // images
    keyed = matmul(normed, wkv).astype(BF16)
    other = swap(keyed)
    queries = matmul(normed, wq).astype(BF16)
    one, two = row_block(slots, width), row_block(slots, 2 * width)
    line = whole_block((1, width))
    after, next_normed, attended = pl.pallas_call(
        attend_kernel,
        grid=(images,),
        in_specs=[
            pl.BlockSpec(memory_space=pltpu.SMEM),
            one,
            two,
            two,
            whole_block((width, width)),
            line,
            one,
            line,
            line,
        ],
        out_specs=[one, one, one],
        out_shape=[
            jax.ShapeDtypeStruct((rows, width), F32),
            jax.ShapeDtypeStruct((rows, width), BF16),
            jax.ShapeDtypeStruct((rows, width), BF16),
        ],
        compiler_params=PARAMS,
        cost_estimate=FORWARD_COST,
        name="attend",
    )(counts, queries, keyed, other, out_weight, out_bias, stream, gain, bias)
    return after, next_normed, (queries, keyed, other, attended)


def attend_backward(stream, low, kept, counts, gain, wq, wkv, out_weight, hold=lambda v: v):
    queries, keyed, other, attended = kept
    rows, width = stream.shape
    images = counts.shape[0]
    slots = rows // images
    one, two = row_block(slots, width), row_block(slots, 2 * width)
    grad_q, grad_own, grad_other = pl.pallas_call(
        attend_back_kernel,
        grid=(images,),
        in_specs=[
            pl.BlockSpec(memory_space=pltpu.SMEM),
            one,
            whole_block((width, width)),
            one,
            two,
            two,
        ],
        out_specs=[one, two, two],
        out_shape=[
            jax.ShapeDtypeStruct((rows, width), BF16),
            jax.ShapeDtypeStruct((rows, 2 * width), F32),
            jax.ShapeDtypeStruct((rows, 2 * width), BF16),
        ],
        compiler_params=PARAMS,
        cost_estimate=BACKWARD_COST,
        name="attend_back",
    )(counts, low, out_weight, queries, keyed, other)
    grad_other = hold(grad_other)
    together = jnp.concatenate([grad_q, grad_own.astype(BF16), grad_other], axis=1)
    together = lax.all_to_all(
        jnp.stack([together, together]), "context", split_axis=0, concat_axis=0, tiled=True
    )
    together = lax.dynamic_index_in_dim(
        together, 1 - lax.axis_index("context"), 0, keepdims=False
    )
    partial = times_transpose(grad_q, wq)
    arrived = together[:, 3 * width :].astype(F32)
    grad_kv = (grad_own + arrived).astype(BF16)
    other_kv = (together[:, width : 3 * width].astype(F32) + grad_other.astype(F32)).astype(BF16)
    grad_normed = partial + times_transpose(grad_kv, wkv)
    grad_stream, unit_grad = norm_backward(stream, grad_normed, gain)
    both_q = both_rows(grad_q, together[:, :width])
    both_kv = both_rows(grad_kv, other_kv)
    return grad_stream, both_q, both_kv, unit_grad, grad_normed


def on_device(
    inputs,
    counts,
    routes,
    cotangent,
    gain1,
    bias1,
    project1,
    output1,
    offset1,
    gain2,
    bias2,
    expand,
    expand_bias,
    shrink,
    shrink_bias,
    gain3,
    bias3,
    project2,
    output2,
    offset2,
    gain4,
    bias4,
    router,
    hidden_weight,
    hidden_bias,
    return_weight,
    return_bias,
):
    images, slots, width = inputs.shape[2:]
    rows = images * slots
    side = lax.axis_index("context")
    count_experts = router.shape[1]

    vectors = (gain1, bias1, offset1, gain2, bias2, shrink_bias, gain3, bias3, offset2, gain4, bias4)
    count = len(vectors)
    small = jnp.concatenate(
        [
            router,
            jnp.concatenate(vectors).reshape(count, 6).T,
            jnp.zeros((6, 128 - count_experts - count), BF16),
        ],
        axis=1,
    )
    first_a = gather_small(project1)
    first_b = gather_small(jnp.concatenate([output1, small], axis=1))
    bulk = gather_small(jnp.concatenate([expand, project2, output2], axis=1))
    tall = gather_small(
        jnp.concatenate([shrink, jnp.pad(expand_bias[:, None], ((0, 0), (0, 127)))], axis=1)
    )
    tall_width = tall.shape[1]
    bulk = lax.all_gather(
        jnp.concatenate([bulk] + [tall[24 * q : 24 * q + 24] for q in range(4)], axis=1),
        ("context", "x", "z"),
        axis=0,
        tiled=True,
    )
    first_a = gather_rest(first_a, "zx")
    first_b = gather_rest(first_b, "xz")
    other_a, other_b = swap(first_a), swap(first_b)
    wq_one = join_sides(first_a[:, :width], other_a[:, :width], side)
    wkv_one = join_sides(first_a[:, width:], other_a[:, width:], side)
    outer_one = join_sides(first_b[:, :width], other_b[:, :width], side)
    small_full = join_sides(first_b[:, width:], other_b[:, width:], side)
    expand_full = bulk[:, : 4 * width]
    wq_two = bulk[:, 4 * width : 5 * width]
    wkv_two = bulk[:, 5 * width : 7 * width]
    outer_two = bulk[:, 7 * width : 8 * width]
    tall_cut = [
        bulk[:, 8 * width + q * tall_width : 8 * width + (q + 1) * tall_width].reshape(
            32, 24, tall_width
        )
        for q in range(4)
    ]
    shrink_full = jnp.stack([cut[:, :, :width] for cut in tall_cut], axis=1).reshape(-1, width)
    shift_full = jnp.stack([cut[:, :, width:] for cut in tall_cut], axis=1).reshape(-1, 128)
    router_full = small_full[:, :count_experts]
    pick = (
        lax.broadcasted_iota(jnp.int32, (16, 128), 1)
        == lax.broadcasted_iota(jnp.int32, (16, 128), 0) + count_experts
    ).astype(BF16)
    lanes = times_transpose(pick, small_full)
    (
        gain_one,
        bias_one,
        offset_one,
        gain_two,
        bias_two,
        shrink_shift,
        gain_three,
        bias_three,
        offset_two,
        gain_four,
        bias_four,
    ) = [lanes[i : i + 1] for i in range(count)]
    first_lane = (lax.broadcasted_iota(jnp.int32, (8, 128), 1) == 0).astype(BF16)
    expand_shift = times_transpose(first_lane, shift_full)[:1]

    stream = inputs.reshape(rows, width).astype(F32)
    own_count = counts.reshape(images)
    slot_iota = jnp.arange(slots, dtype=jnp.int32)
    row_valid = (slot_iota[None, :] < own_count[:, None]).reshape(rows, 1)
    valid = row_valid.astype(F32)
    capacity = max(2, 2 * rows // count_experts + 1)
    places = count_experts * capacity
    chosen = routes.reshape(rows, 2)
    expert_iota = jnp.arange(count_experts, dtype=jnp.int32)
    hots = [chosen[:, k : k + 1] == expert_iota for k in range(2)]
    row_hot = (hots[0] | hots[1]).astype(BF16)
    earlier_rows = (
        lax.broadcasted_iota(jnp.int32, (rows, rows), 1)
        < lax.broadcasted_iota(jnp.int32, (rows, rows), 0)
    ).astype(BF16)
    earlier = matmul(earlier_rows, row_hot)
    place_iota = lax.broadcasted_iota(jnp.int32, (rows, places), 1)
    goes = []
    for k in range(2):
        slot = jnp.sum(jnp.where(hots[k], earlier, 0.0), axis=-1, keepdims=True).astype(jnp.int32)
        goes.append(place_iota == chosen[:, k : k + 1] * capacity + slot)
    dispatch = [g.astype(BF16) for g in goes]
    row_dispatch = (goes[0] | goes[1]).astype(BF16)

    normed_one = norm_forward(stream, gain_one, bias_one)
    after_one, normed_two, kept_one = attend_forward(
        stream, normed_one, own_count, wq_one, wkv_one, outer_one, offset_one, gain_two, bias_two
    )
    hidden_two, slope_two = gelu_both(matmul(normed_two, expand_full) + expand_shift)
    hidden_two = hidden_two.astype(BF16)
    after_two = after_one + matmul(hidden_two, shrink_full) + shrink_shift
    normed_three = norm_forward(after_two, gain_three, bias_three)
    after_three, normed, kept_three = attend_forward(
        after_two,
        normed_three,
        own_count,
        wq_two,
        wkv_two,
        outer_two,
        offset_two,
        gain_four,
        bias_four,
    )
    halves = [normed_one, kept_one[3], normed_two, hidden_two, normed_three, kept_three[3], normed]
    arriving = swap(jnp.concatenate([own_half(v, 1 - side) for v in halves], axis=1))
    lefts, at = [], 0
    for v in halves:
        half = v.shape[1] // 2
        lefts.append(both_rows(own_half(v, side), arriving[:, at : at + half]))
        at += half
    left_one, left_out_one, left_two, left_hidden, left_three, left_out_three, left_four = lefts
    logits = matmul(normed, router_full)
    picked = [
        jnp.sum(jnp.where(hots[k], logits, 0.0), axis=-1, keepdims=True) for k in range(2)
    ]
    top = jnp.maximum(picked[0], picked[1])
    powers = [jnp.exp(p - top) for p in picked]
    shares = [p / (powers[0] + powers[1]) for p in powers]
    gates = [s * valid for s in shares]

    low_four = jnp.where(row_valid, cotangent.reshape(rows, width), jnp.zeros((), BF16))
    grad_four = low_four.astype(F32)
    place_gate = jnp.sum(
        jnp.where(goes[0], gates[0], 0.0) + jnp.where(goes[1], gates[1], 0.0), axis=0
    )
    sent = contract_rows(row_dispatch, normed).astype(BF16)
    grad_sent = (contract_rows(row_dispatch, low_four) * place_gate[:, None]).astype(BF16)
    arrived = lax.all_to_all(
        jnp.concatenate([sent, grad_sent], axis=1).reshape(count_experts, capacity, 2 * width),
        ("x", "z", "y"),
        split_axis=0,
        concat_axis=0,
        tiled=True,
    ).reshape(places, 2 * width)
    arrived = jnp.concatenate([arrived, swap(arrived)], axis=0)
    expert_rows, grad_rows = arrived[:, :width], arrived[:, width:]
    in_weight, out_weight = hidden_weight[0], return_weight[0]
    hidden, slope = gelu_both(matmul(expert_rows, in_weight) + hidden_bias[0].astype(F32))
    hidden = hidden.astype(BF16)
    grad_before = (slope * times_transpose(grad_rows, out_weight)).astype(BF16)
    result = jnp.concatenate(
        [matmul(hidden, out_weight), times_transpose(grad_before, in_weight)], axis=1
    )
    result = result[:places] + swap(result[places:].astype(BF16)).astype(F32)
    back = jnp.concatenate(
        [result[:, :width] + return_bias[0].astype(F32), result[:, width:]], axis=1
    ).astype(BF16)
    wide_back = lax.all_to_all(
        back.reshape(count_experts, capacity, 2 * width),
        ("x", "z", "y"),
        split_axis=0,
        concat_axis=0,
        tiled=True,
    ).reshape(places, 2 * width)
    grad_return_bias = jnp.sum(grad_rows.astype(F32), axis=0)
    grad_return = contract_rows(hidden, grad_rows)
    grad_hidden_bias = jnp.sum(grad_before.astype(F32), axis=0)
    grad_hidden_weight = contract_rows(expert_rows, grad_before)
    back, grad_return, grad_hidden_weight = lax.optimization_barrier(
        (wide_back, grad_return, grad_hidden_weight)
    )
    pair_out = [matmul(dispatch[k], back[:, :width]) for k in range(2)]
    mixture = gates[0] * pair_out[0] + gates[1] * pair_out[1]
    outputs = ((after_three + mixture) * valid).astype(BF16).reshape(inputs.shape)

    grad_gates = [jnp.sum(grad_four * pair_out[k], axis=-1, keepdims=True) for k in range(2)]
    centre = shares[0] * grad_gates[0] + shares[1] * grad_gates[1]
    grad_picked = [valid * shares[k] * (grad_gates[k] - centre) for k in range(2)]
    grad_logits = (
        jnp.where(hots[0], grad_picked[0], 0.0) + jnp.where(hots[1], grad_picked[1], 0.0)
    ).astype(BF16)
    grad_normed = times_transpose(grad_logits, router_full) + matmul(
        row_dispatch, back[:, width:]
    )
    grad_flat, unit_four = norm_backward(after_three, grad_normed, gain_four)
    grad_three = grad_four + grad_flat
    wide_logits = jnp.pad(grad_logits, ((0, 0), (0, 128 - count_experts)))

    low_three = grad_three.astype(BF16)
    low_logits = swap(jnp.concatenate([low_three, wide_logits], axis=1))
    grad_part, both_q, both_kv, unit_three, grad_normed_three = attend_backward(
        after_two, low_three, kept_three, own_count, gain_three, wq_two, wkv_two, outer_two
    )
    grad_two = grad_three + grad_part
    low_two = grad_two.astype(BF16)
    other_low_two = swap(low_two)
    sums_a = row_sums([unit_four, grad_normed, low_three, unit_three, grad_normed_three], side)
    job_a = Job(
        [
            contract_rows(left_three, both_q),
            contract_rows(left_three, both_kv),
            contract_rows(left_out_three, both_rows(low_three, low_logits[:, :width])),
            contract_rows(left_four, both_rows(wide_logits, low_logits[:, width:]))
            + jnp.roll(sums_a, count_experts, axis=1),
        ],
        "xzy",
    )
    low_two = tie_jobs(low_two, job_a)
    grad_before_two = (slope_two * times_transpose(low_two, shrink_full)).astype(BF16)
    other_before_two = swap(grad_before_two)
    sums_b = contract_rows(
        grad_before_two,
        (lax.broadcasted_iota(jnp.int32, (rows, 128), 1) == 0).astype(BF16),
    )
    half = sums_b.shape[0] // 2
    sums_b = lax.dynamic_slice_in_dim(sums_b, side * half, half, 0) + swap(
        lax.dynamic_slice_in_dim(sums_b, (1 - side) * half, half, 0).astype(BF16)
    ).astype(F32)
    job_b = Job([contract_rows(left_hidden, both_rows(low_two, other_low_two)), sums_b], "yzx")
    grad_before_two = tie_jobs(grad_before_two, job_b)
    grad_normed_two = times_transpose(grad_before_two, expand_full)
    grad_part, unit_two = norm_backward(after_one, grad_normed_two, gain_two)
    grad_one = grad_two + grad_part
    low_one = grad_one.astype(BF16)
    other_low_one = swap(low_one)
    job_c = Job(
        [
            contract_rows(left_two, both_rows(grad_before_two, other_before_two)),
            contract_rows(left_out_one, both_rows(low_one, other_low_one)),
            row_sums([low_two, unit_two, grad_normed_two, low_one], side),
        ],
        "zxy",
    )
    low_one = tie_jobs(low_one, job_c, job_a.step())
    grad_part, both_q, both_kv, unit_one, grad_normed_one = attend_backward(
        stream,
        low_one,
        kept_one,
        own_count,
        gain_one,
        wq_one,
        wkv_one,
        outer_one,
        lambda v: tie_jobs(v, job_a.step(), job_b.step(), job_c.step()),
    )
    job_e = Job([contract_rows(left_one, both_q), contract_rows(left_one, both_kv)], "xzy")
    unit_one = tie_jobs(unit_one, job_e)
    job_f = Job([row_sums([unit_one, grad_normed_one], side)], "zxy")
    tie_jobs(job_e.step().now, job_a.step(), job_b.step(), job_c.step(), job_f.step())
    job_c.now = jnp.concatenate([job_c.now, job_f.step().now], axis=1)
    tie_jobs(job_e.step().now, job_a.step(), job_b.step(), job_c.step())
    tie_jobs(job_e.step().now, job_a.step(), job_b.step(), job_c.step())
    tie_jobs(job_e.step().now, job_a.step(), job_b.step(), job_c.step())
    tie_jobs(job_e.step().now, job_b.step(), job_c.step())
    job_e.step()
    sum_a, sum_b, sum_c, sum_e = job_a.now, job_b.now, job_c.now, job_e.now
    grad_inputs = (grad_one + grad_part).reshape(inputs.shape)

    wide = 4 * width
    return (
        outputs,
        grad_inputs,
        sum_c[:, wide + width + 128],
        sum_c[:, wide + width + 129],
        sum_e[:, : 3 * width],
        sum_c[:, wide : wide + width],
        sum_c[:, wide + width + 3],
        sum_c[:, wide + width + 1],
        sum_c[:, wide + width + 2],
        sum_c[:, :wide],
        sum_b[:, width],
        sum_b[:, :width],
        sum_c[:, wide + width],
        sum_a[:, wide + 67],
        sum_a[:, wide + 68],
        sum_a[:, : 3 * width],
        sum_a[:, 3 * width : wide],
        sum_a[:, wide + 66],
        sum_a[:, wide + 64],
        sum_a[:, wide + 65],
        sum_a[:, wide : wide + 64],
        grad_hidden_weight[None],
        grad_hidden_bias[None],
        grad_return[None],
        grad_return_bias[None],
    )


def solution(mesh):
    chips = ("x", "z", "y")
    finer = Mesh(mesh.devices.reshape(2, 4, 4, 4), ("context",) + chips)
    vector = P(("context",) + chips)
    matrix = P(("context",) + chips, None)
    token = P(chips, "context", None, None, None)
    expert = (
        P(chips, None, "context"),
        P(chips, "context"),
        P(chips, "context", None),
        P(chips, None),
    )
    dense = (
        (vector, vector, matrix, matrix, vector)
        + (vector, vector, matrix, vector, matrix, vector)
        + (vector, vector, matrix, matrix, vector)
        + (vector, vector, matrix)
    )
    return jax.shard_map(
        on_device,
        mesh=finer,
        in_specs=(token, P(chips, "context", None), token, token) + dense + expert,
        out_specs=(token, token) + dense + expert,
        check_vma=False,
    )
```
